256 devices in a mesh: ta: 32 (over z, x_lo, core), dev: 8 (over y, x_hi).
Axes of the slice: x: 4 (x_hi: 2, x_lo: 2; x = x_hi * 2 + x_lo), y: 4, z: 8, core: 2. Of those that a mesh axis runs over, the one named last changes fastest.
Arguments:
- raw_integrals: bfloat16 [512, 64, 36864], P(('ta', 'dev')), may hold values from -6 to 6
- metric: bfloat16 [512, 64, 64], P(('ta', 'dev')), may hold values from -0.125 to 0.125
- aux_list: int32 [512, 3], P(('ta', 'dev')), may hold values from 0 to 1023, as said below
- density_list: int32 [1024, 8], replicated, may hold values from 0 to 1023, as said below
- density_blocks: bfloat16 [1024, 8, 64, 64], P('ta', 'dev'), may hold values from -0.4375 to 0.4375
Outputs:
- exchange: float32 [1024, 8, 64, 64], P('ta', 'dev')
The draws below stay inside these ranges and needn't reach their ends.
Inputs may be any that keep to these rules, and one draw needn't show every extreme that they name: `aux_list`: row a names 3 different orbital blocks, all among blocks s to s + 4 taken modulo 1024 for some s from g * 32 - 4 to (g + 1) * 32 - 1, where g = a // 16 is the index along ta of the device holding row a. `density_list`: row r names each of the column blocks r - 3 to r + 4, taken modulo 1024, once, in some order.
All inputs are finite; a program needn't handle non-finite values.
Results may differ from the reference program's by a relative error of at most 0.0065.
Values may be sent and summed in bfloat16 or wider, within the bound.
No kernel may reach another device: no remote copies, remote signals or barrier semaphores. Data moves between devices by JAX's collectives and lax.ppermute only.
A program may use at most 192 MiB of HBM per device.

```python
import jax
import jax.numpy as jnp
from jax import lax

AB = 64
OB = 64
NL = 3
ND = 8
OBD = 32
W = 192
NOB = 1024
NAB = 512


def random_order(key, row_count, candidates):
    scores = jax.random.randint(key, (row_count, candidates), 0, 1 << 20) * candidates
    scores = scores + jnp.arange(candidates, dtype=jnp.int32)[None, :]
    return jnp.argsort(scores, axis=1).astype(jnp.int32)


def draw_aux_list(key, part):
    key = jax.random.fold_in(key, 11)
    key_full, key_low, key_high, key_pick, key_order = jax.random.split(key, 5)
    per_group = NAB * OBD // NOB
    rows = jnp.arange(NAB, dtype=jnp.int32)
    home_index = rows // per_group
    local_index = rows % per_group
    start_full = jax.random.randint(key_full, (NAB,), 0, OBD + NL + 1) - (NL + 1)
    start_low = jax.random.randint(key_low, (NAB,), 0, NL + 1) - (NL + 1)
    start_high = jax.random.randint(key_high, (NAB,), 0, NL + 1) + (OBD - NL - 1)
    start_rel = jnp.where(local_index == 0, start_low, jnp.where(local_index == 1, start_high, start_full))
    span = NL + 2
    scores = jax.random.randint(key_pick, (NAB, span), 0, 1 << 20) * span
    scores = scores + jnp.arange(span, dtype=jnp.int32)[None, :]
    candidate = jnp.arange(span, dtype=jnp.int32)[None, :]
    forced = (local_index[:, None] == 0) & (candidate == 0) | (local_index[:, None] == 1) & (candidate == span - 1)
    scores = jnp.where(forced, -1, scores)
    picked = jnp.argsort(scores, axis=1)[:, :NL].astype(jnp.int32)
    shuffle = random_order(key_order, NAB, NL)
    picked = jnp.take_along_axis(picked, shuffle, axis=1)
    first = home_index * OBD + start_rel
    return ((first[:, None] + picked) % NOB).astype(jnp.int32)


def draw_density_list(key, part):
    key = jax.random.fold_in(key, 12)
    offsets = random_order(key, NOB, ND) - (ND // 2 - 1)
    row_ids = jnp.arange(NOB, dtype=jnp.int32)
    return ((row_ids[:, None] + offsets) % NOB).astype(jnp.int32)


def block_levels(rng, extent, cuts, smallest, high):
    loudness = 1.0
    for axis_at, parts in cuts:
        heights = jax.random.uniform(jax.random.fold_in(jax.random.fold_in(rng, 6), axis_at), (parts,), jnp.float32, smallest / len(cuts), high / len(cuts))
        loudness = loudness * jnp.repeat(jnp.exp(heights), extent[axis_at] // parts).reshape((-1,) + (1,) * (len(extent) - 1 - axis_at))
    return loudness


def normal_values(stream_key, extent, spread, bound, cuts=(), kind=jnp.bfloat16):
    level = block_levels(stream_key, extent, cuts, -0.22, 0.18) if cuts else 1.0
    drawn = jax.random.normal(stream_key, extent, jnp.float32) * spread * level
    return jnp.minimum(jnp.maximum(drawn, -bound), bound).astype(kind)


def setup_inputs(seed: int = 0) -> dict:
    streams_of = jax.random.split(jax.random.key(seed), 6)
    raw_integrals = normal_values(streams_of[0], (NAB, AB, W * W), 1.0, 6.0, ((0, 256),))
    metric = normal_values(streams_of[1], (NAB, AB, AB), (40 * AB) ** -0.5, 0.125, ((0, 256),))
    aux_list = draw_aux_list(jax.random.fold_in(streams_of[5], 71), 0)
    density_list = draw_density_list(jax.random.fold_in(streams_of[5], 71), 0)
    density_blocks = normal_values(streams_of[4], (NOB, ND, OB, OB), (NL * OB) ** -0.5, 0.4375, ((0, 32), (1, 8)))
    return {"raw_integrals": raw_integrals, "metric": metric, "aux_list": aux_list, "density_list": density_list, "density_blocks": density_blocks}


def block_terms(integral_block, metric_block, orbital_ids, column_ids, density_rows):
    functions = integral_block.shape[0]
    orbitals = density_rows.shape[-1]
    listed = orbital_ids.shape[0]
    window = listed * orbitals
    fitted = jnp.dot(metric_block, integral_block, preferred_element_type=jnp.float32)
    fitted = fitted.astype(jnp.bfloat16).reshape(functions, window, window)
    matches = (column_ids[:, None, :] == orbital_ids[None, :, None]).astype(jnp.float32)
    window_density = jnp.einsum("ijk,ikab->iajb", matches, density_rows.astype(jnp.float32))
    window_density = window_density.astype(jnp.bfloat16).reshape(window, window)
    mixed = jnp.dot(fitted.reshape(functions * window, window), window_density, preferred_element_type=jnp.float32)
    mixed = mixed.astype(jnp.bfloat16).reshape(functions, window, window)
    contribution = lax.dot_general(mixed, fitted, (((0, 2), (0, 2)), ((), ())), preferred_element_type=jnp.float32)
    return jnp.einsum("ijk,iajb->ikab", matches, contribution.reshape(listed, orbitals, listed, orbitals))


def reference(raw_integrals, metric, aux_list, density_list, density_blocks):
    def one_block(totals, operands):
        integral_block, metric_block, orbital_ids = operands
        pieces = block_terms(integral_block, metric_block, orbital_ids, density_list[orbital_ids], density_blocks[orbital_ids])
        return totals.at[orbital_ids].add(pieces), None

    start_totals = jnp.zeros(density_blocks.shape, jnp.float32)
    exchange, unused = lax.scan(one_block, start_totals, (raw_integrals, metric, aux_list))
    return exchange
```

```python
import functools

import jax
import jax.numpy as jnp
from jax import lax
from jax.experimental import pallas as pl
from jax.experimental.pallas import tpu as pltpu
from jax.sharding import PartitionSpec as P

BF16 = jnp.bfloat16
F32 = jnp.float32
HALO = 4
VMEM_LIMIT = 50 * 2**20


def whole(shape):
    return pl.BlockSpec(shape, lambda *_: (0,) * len(shape))


def fit_kernel(rows, stride, window, metric_ref, raw_ref, *refs):
    out_ref, low, high = refs[-3:]
    aux = metric_ref.shape[1]
    metric = metric_ref[0]
    for pair in range(rows // 2):
        lanes = pl.ds(pair * 2 * window, 2 * window)
        both = jnp.dot(metric, raw_ref[0, :, lanes], preferred_element_type=F32)
        turned = pltpu.roll(both, window, axis=1)
        for half, values in enumerate((both, turned)):
            at = pl.ds(2 * pair + half, aux, stride=stride)
            low[at, :] = values[:, :128]
            high[at, :] = values[:, 128:256]
    out_ref[0, :, :, :128] = low[...].reshape(aux, stride, 128)[:, :rows].astype(BF16)
    rest = window - 128
    upper = high[:, :rest].reshape(aux, stride, rest)[:, :rows]
    out_ref[0, :, :, 128:] = upper.astype(BF16)


def fit(raw, metric, window, which, onto=None, rows=96):
    count, aux, merged = raw.shape
    stride = rows + 8
    operands = [metric, raw]
    in_specs = [
        pl.BlockSpec((1, aux, aux), lambda c: (which, 0, 0)),
        pl.BlockSpec((1, aux, rows * window), lambda c: (which, 0, c)),
    ]
    if onto is not None:
        operands.append(onto)
        in_specs.append(pl.BlockSpec(memory_space=pl.ANY))
    return pl.pallas_call(
        functools.partial(fit_kernel, rows, stride, window),
        grid=(window // rows,),
        in_specs=in_specs,
        out_specs=pl.BlockSpec((1, aux, rows, window), lambda c: (which, 0, c, 0)),
        out_shape=jax.ShapeDtypeStruct((count, aux, window, window), BF16),
        scratch_shapes=[pltpu.VMEM((aux * stride, 128), F32)] * 2,
        input_output_aliases={} if onto is None else {2: 0},
        compiler_params=pltpu.CompilerParams(vmem_limit_bytes=VMEM_LIMIT),
        cost_estimate=pl.CostEstimate(
            flops=2 * aux * aux * merged, bytes_accessed=5 * aux * merged, transcendentals=0
        ),
        name="fit",
    )(*operands)


def pack_kernel(rows, own_ref, before_ref, after_ref, out_ref, near):
    slab = own_ref.shape[0]
    near[:HALO] = before_ref[...]
    near[HALO : HALO + slab] = own_ref[...]
    near[HALO + slab :] = after_ref[...]
    peers, listed = out_ref.shape[:2]
    for peer in range(peers):
        for i in range(listed):
            at = peer * 2 * listed + i
            pair = (near[rows[at]], near[rows[at + listed]])
            out_ref[peer, i] = jnp.concatenate(pair, axis=1)


def pack(rows, own, before, after, peers, listed):
    slab, orbitals = own.shape[:2]
    shape = (peers, listed, orbitals, 2 * orbitals)
    return pl.pallas_call(
        pack_kernel,
        grid_spec=pltpu.PrefetchScalarGridSpec(
            num_scalar_prefetch=1,
            grid=(1,),
            in_specs=[whole(own.shape), whole(before.shape), whole(after.shape)],
            out_specs=whole(shape),
            scratch_shapes=[pltpu.VMEM((slab + 2 * HALO, orbitals, orbitals), BF16)],
        ),
        out_shape=jax.ShapeDtypeStruct(shape, BF16),
        cost_estimate=pl.CostEstimate(flops=0, bytes_accessed=2**20, transcendentals=0),
        name="pack",
    )(rows, own, before, after)


def mix_kernel(part, steps, slots, fit_ref, recv_ref, out_ref, dens, acc):
    a, t = pl.program_id(0), pl.program_id(1)
    listed, ob = recv_ref.shape[1:3]
    window = listed * ob

    @pl.when((a == 0) & (t == 0))
    def _():
        out_ref[...] = jnp.zeros_like(out_ref)

    @pl.when(t == 0)
    def _():
        for i in range(listed):
            blocks = []
            for j in range(listed):
                slot = slots[(a * listed + i) * listed + j]
                pair = recv_ref[jnp.maximum(slot, 0), i].astype(F32)
                block = jnp.where(a == 0, pair[:, :ob], pair[:, ob:])
                blocks.append(jnp.where(slot >= 0, block, 0.0))
            dens[i * ob : (i + 1) * ob, :] = jnp.concatenate(blocks, axis=1).astype(BF16)
        acc[...] = jnp.zeros_like(acc)

    fitted = fit_ref[0].reshape(part * window, window)
    mixed = jnp.dot(fitted, dens[...], preferred_element_type=F32).astype(BF16)
    total = None
    for q in range(part):
        term = lax.dot_general(
            mixed[q * window : (q + 1) * window],
            fit_ref[0, q],
            (((1,), (1,)), ((), ())),
            preferred_element_type=F32,
        )
        total = term if total is None else total + term
    acc[...] += total

    for half in range(2):

        @pl.when((t == steps - 1) & (a == half))
        def _():
            for i in range(listed):
                for j in range(listed):
                    slot = slots[(half * listed + i) * listed + j]
                    block = acc[i * ob : (i + 1) * ob, j * ob : (j + 1) * ob]

                    @pl.when(slot >= 0)
                    def _():
                        out_ref[slot, i, :, half * ob : (half + 1) * ob] = block.astype(BF16)


def mix(slots, fitted, received, part=32):
    count, aux, window, _ = fitted.shape
    shape = received.shape
    return pl.pallas_call(
        functools.partial(mix_kernel, part, aux // part),
        grid_spec=pltpu.PrefetchScalarGridSpec(
            num_scalar_prefetch=1,
            grid=(count, aux // part),
            in_specs=[
                pl.BlockSpec((1, part, window, window), lambda a, t, s: (a, t, 0, 0)),
                whole(shape),
            ],
            out_specs=whole(shape),
            scratch_shapes=[pltpu.VMEM((window, window), BF16), pltpu.VMEM((window, window), F32)],
        ),
        out_shape=jax.ShapeDtypeStruct(shape, BF16),
        compiler_params=pltpu.CompilerParams(vmem_limit_bytes=VMEM_LIMIT),
        cost_estimate=pl.CostEstimate(
            flops=4 * count * aux * window**3,
            bytes_accessed=2 * count * aux * window**2,
            transcendentals=0,
        ),
        name="mix",
    )(slots, fitted, received)


def sum_kernel(rows, terms_ref, own_ref, low_ref, high_ref, total):
    peers, listed, ob, lanes = terms_ref.shape
    slab = own_ref.shape[0]
    first = lax.broadcasted_iota(jnp.int32, (ob, lanes), 1) < ob
    total[...] = jnp.zeros_like(total)
    for peer in range(peers):
        for i in range(listed):
            at = peer * 2 * listed + i
            pair = terms_ref[peer, i].astype(F32)
            total[rows[at]] += jnp.where(first, pair, 0.0)
            total[rows[at + listed]] += jnp.where(first, 0.0, pair)

    def folded(rows_of):
        return rows_of[:, :, :ob] + rows_of[:, :, ob:]

    low_ref[...] = folded(total[:HALO])
    high_ref[...] = folded(total[HALO + slab :])
    own_ref[...] = folded(total[HALO : HALO + slab])


def sum_terms(rows, terms, slab):
    ob, lanes = terms.shape[2:]
    shapes = [(slab, ob, ob), (HALO, ob, ob), (HALO, ob, ob)]
    return pl.pallas_call(
        sum_kernel,
        grid_spec=pltpu.PrefetchScalarGridSpec(
            num_scalar_prefetch=1,
            grid=(1,),
            in_specs=[whole(terms.shape)],
            out_specs=[whole(s) for s in shapes],
            scratch_shapes=[pltpu.VMEM((slab + 2 * HALO, ob, lanes), F32)],
        ),
        out_shape=[jax.ShapeDtypeStruct(s, F32) for s in shapes],
        cost_estimate=pl.CostEstimate(flops=0, bytes_accessed=2**21, transcendentals=0),
        name="sum_terms",
    )(rows, terms)


def edge_kernel(own_ref, before_ref, after_ref, out_ref):
    @pl.when(pl.program_id(0) == 0)
    def _():
        out_ref[...] = own_ref[...] + before_ref[...]

    @pl.when(pl.program_id(0) == 1)
    def _():
        out_ref[...] = own_ref[...] + after_ref[...]


def add_edges(own, before, after):
    slab, ob = own.shape[:2]
    last = slab // HALO - 1
    edge = pl.BlockSpec((HALO, ob, ob), lambda e: (e * last, 0, 0))
    return pl.pallas_call(
        edge_kernel,
        grid=(2,),
        in_specs=[edge, whole(before.shape), whole(after.shape)],
        out_specs=edge,
        out_shape=jax.ShapeDtypeStruct(own.shape, F32),
        input_output_aliases={0: 0},
        name="add_edges",
    )(own, before, after)


def ring(value, axis, steps):
    count = lax.axis_size(axis)
    pairs = [(source, (source + steps) % count) for source in range(count)]
    return lax.ppermute(value, axis, pairs)


def per_device(raw_integrals, metric, aux_list, density_list, density_blocks):
    slab, _, ob = density_blocks.shape[:3]
    count, listed = aux_list.shape
    peers = lax.axis_size("dev")
    block_count = slab * lax.axis_size("ta")
    window = listed * ob
    first_block = lax.axis_index("ta") * slab - HALO
    own = density_blocks.reshape(slab, ob, ob)

    names = jnp.broadcast_to(aux_list.reshape(1, -1), (peers, count * listed))
    names = lax.all_to_all(names, "dev", 0, 0, tiled=True)
    rows = ((names - first_block) % block_count).reshape(-1)
    before = ring(own[-HALO:], "ta", 1)
    after = ring(own[:HALO], "ta", -1)

    columns = density_list[aux_list]
    match = columns[:, :, None, :] == aux_list[:, None, :, None]
    places = jnp.arange(1, columns.shape[-1] + 1, dtype=jnp.int32)
    slots = (jnp.sum(jnp.where(match, places, 0), axis=-1) - 1).reshape(-1)

    fitted = fit(raw_integrals, metric, window, 0)
    packed = pack(rows, own, before, after, peers, listed)
    received = lax.all_to_all(packed, "dev", 0, 0, tiled=True)
    fitted = fit(raw_integrals, metric, window, 1, fitted)
    terms = mix(slots, fitted, received)
    terms = lax.all_to_all(terms, "dev", 0, 0, tiled=True)
    totals, low, high = sum_terms(rows, terms, slab)
    from_before = ring(high, "ta", 1)
    from_after = ring(low, "ta", -1)
    return add_edges(totals, from_before, from_after).reshape(density_blocks.shape)


def solution(mesh):
    placed = (
        P(("ta", "dev"), None, None),
        P(("ta", "dev"), None, None),
        P(("ta", "dev"), None),
        P(),
        P("ta", "dev", None, None),
    )
    return jax.shard_map(
        per_device,
        mesh=mesh,
        in_specs=placed,
        out_specs=P("ta", "dev", None, None),
        check_vma=False,
    )
```

```python
import functools

import jax
import jax.numpy as jnp
from jax import lax
from jax.experimental import pallas as pl
from jax.experimental.pallas import tpu as pltpu
from jax.sharding import PartitionSpec as P

BF16 = jnp.bfloat16
F32 = jnp.float32
HALO = 4
PAIRS = 32
STEP = 32
DEPTH = 3
PIECE = 16
PARTS = ((16, 16, 32), (32, 32))
VMEM_LIMIT = 56 * 2**20


def in_vmem():
    return pl.BlockSpec(memory_space=pltpu.VMEM)


def in_smem():
    return pl.BlockSpec(memory_space=pltpu.SMEM)


def anywhere():
    return pl.BlockSpec(memory_space=pl.ANY)


def fit_kernel(pairs, stride, names, columns, metric_ref, raw_ref, out_ref, slots, *refs):
    held, made, in_sems, out_sems, *parts = refs
    count, aux = metric_ref.shape[:2]
    rows, width = out_ref.shape[2:]
    pieces = rows // STEP
    total = count * pieces
    chunks = count * rows // pairs

    def arriving(k):
        slot = k % DEPTH
        lanes = pl.ds(k % pieces * STEP * width, STEP * width)
        there = raw_ref.at[k // pieces, :, lanes]
        return pltpu.make_async_copy(there, held.at[slot], in_sems.at[slot])

    def leaving(n):
        a, start = divmod(n * pairs, rows)
        there = out_ref.at[a, :, pl.ds(start, pairs), :]
        return pltpu.make_async_copy(made.at[n % 2], there, out_sems.at[n % 2])

    for k in range(DEPTH):
        arriving(k).start()
    stored, listed = columns.shape[0], names.shape[1]
    for a in range(count):
        for i in range(listed):
            row = names[a, i]
            for j in range(listed):
                column = names[a, j]
                slot = jnp.int32(-1)
                for k in range(stored):
                    slot = jnp.where(columns[k, row] == column, k, slot)
                slots[(a * listed + i) * listed + j] = slot
    for n in range(chunks):
        metric = metric_ref[n * pairs // rows]
        for r in range(pairs):
            k, at = divmod(n * pairs + r, STEP)
            if at == 0:
                arriving(k).wait()
            lanes = pl.ds(at * width, width)
            both = jnp.dot(metric, held[k % DEPTH, :, lanes], preferred_element_type=F32)
            for v, part in enumerate(parts):
                part[pl.ds(r, aux, stride=stride), :] = both[:, v * 128 : (v + 1) * 128]
            if at == STEP - 1 and k + DEPTH < total:
                arriving(k + DEPTH).start()
        if n >= 2:
            leaving(n - 2).wait()
        for v, part in enumerate(parts):
            values = part[...].reshape(aux, stride, 128)[:, :pairs]
            made[n % 2, :, :, v * 128 : (v + 1) * 128] = values.astype(BF16)
        leaving(n).start()
    for n in range(chunks - 2, chunks):
        leaving(n).wait()


def fit(names, columns, metric, raw, window):
    count, aux, merged = raw.shape
    listed = names.shape[1]
    stride = PAIRS + 8
    width = 2 * window
    return pl.pallas_call(
        functools.partial(fit_kernel, PAIRS, stride),
        in_specs=[in_smem(), in_smem(), in_vmem(), anywhere()],
        out_specs=[anywhere(), in_smem()],
        out_shape=[
            jax.ShapeDtypeStruct((count, aux, window // 2, width), BF16),
            jax.ShapeDtypeStruct((count * listed * listed,), jnp.int32),
        ],
        scratch_shapes=[
            pltpu.VMEM((DEPTH, aux, STEP * width), BF16),
            pltpu.VMEM((2, aux, PAIRS, width), BF16),
            pltpu.SemaphoreType.DMA((DEPTH,)),
            pltpu.SemaphoreType.DMA((2,)),
        ]
        + [pltpu.VMEM((aux * stride, 128), F32)] * (width // 128),
        compiler_params=pltpu.CompilerParams(vmem_limit_bytes=VMEM_LIMIT),
        cost_estimate=pl.CostEstimate(
            flops=2 * count * aux * aux * merged,
            bytes_accessed=4 * count * aux * merged,
            transcendentals=0,
        ),
        name="fit",
    )(names, columns, metric, raw)


def pack_kernel(rows, own_ref, before_ref, after_ref, out_ref, near):
    slab = own_ref.shape[0]
    near[:HALO] = before_ref[...]
    near[HALO : HALO + slab] = own_ref[...]
    near[HALO + slab :] = after_ref[...]
    peers, listed = out_ref.shape[:2]
    for peer in range(peers):
        for i in range(listed):
            pair = [near[rows[peer, a, i]] for a in range(2)]
            out_ref[peer, i] = jnp.concatenate(pair, axis=1)


def pack(rows, own, before, after):
    slab, ob = own.shape[:2]
    peers, _, listed = rows.shape
    return pl.pallas_call(
        pack_kernel,
        in_specs=[in_smem(), in_vmem(), in_vmem(), in_vmem()],
        out_specs=in_vmem(),
        scratch_shapes=[pltpu.VMEM((slab + 2 * HALO, ob, ob), BF16)],
        out_shape=jax.ShapeDtypeStruct((peers, listed, ob, 2 * ob), BF16),
        cost_estimate=pl.CostEstimate(flops=0, bytes_accessed=2**20, transcendentals=0),
        name="pack",
    )(rows, own, before, after)


def mix_kernel(slots, fit_ref, recv_ref, out_ref, dens, held, sems):
    count, aux, pairs, width = fit_ref.shape
    listed, ob = recv_ref.shape[1:3]
    window = width // 2
    total = count * aux // PIECE

    def arriving(n):
        at = (n * PIECE // aux, pl.ds(n * PIECE % aux, PIECE))
        return pltpu.make_async_copy(fit_ref.at[at], held.at[at], sems.at[n])

    for n in range(DEPTH):
        arriving(n).start()
    out_ref[...] = jnp.zeros_like(out_ref)
    row = lax.broadcasted_iota(jnp.int32, (window, window), 0)
    column = lax.broadcasted_iota(jnp.int32, (window, window), 1)
    turn = (lax.rem(row, 2) * pairs + lax.div(row, 2) == column).astype(BF16)
    across = (((1,), (1,)), ((), ()))
    for a in range(count):
        for i in range(listed):
            blocks = []
            for j in range(listed):
                slot = slots[(a * listed + i) * listed + j]
                block = recv_ref[jnp.maximum(slot, 0), i, :, a * ob : (a + 1) * ob]
                blocks.append(jnp.where(slot >= 0, block, jnp.zeros_like(block)))
            dens[a, i * ob : (i + 1) * ob, :] = jnp.concatenate(blocks, axis=1)
    for a in range(count):
        density = dens[a]
        summed = None
        done = 0
        for part in PARTS[a]:
            for n in range((a * aux + done) // PIECE, (a * aux + done + part) // PIECE):
                arriving(n).wait()
                if n + DEPTH < total:
                    arriving(n + DEPTH).start()
            rows = held[a, pl.ds(done, part)]
            fitted = jnp.concatenate([rows[..., :window], rows[..., window:]], axis=1)
            fitted = fitted.reshape(part * window, window)
            mixed = jnp.dot(fitted, density, preferred_element_type=F32).astype(BF16)
            for q in range(part):
                at = slice(q * window, (q + 1) * window)
                term = lax.dot_general(
                    mixed[at], fitted[at], across, preferred_element_type=F32
                )
                summed = term if summed is None else summed + term
            done += part

        half = lax.dot_general(
            summed.astype(BF16), turn, across, preferred_element_type=F32
        ).astype(BF16)
        terms = jnp.dot(turn, half, preferred_element_type=F32).astype(BF16)
        for i in range(listed):
            for j in range(listed):
                slot = slots[(a * listed + i) * listed + j]
                block = terms[i * ob : (i + 1) * ob, j * ob : (j + 1) * ob]

                @pl.when(slot >= 0)
                def _():
                    out_ref[slot, i, :, a * ob : (a + 1) * ob] = block


def mix(slots, fitted, received):
    count, aux, pairs, width = fitted.shape
    window = width // 2
    return pl.pallas_call(
        mix_kernel,
        in_specs=[in_smem(), anywhere(), in_vmem()],
        out_specs=in_vmem(),
        scratch_shapes=[
            pltpu.VMEM((count, window, window), BF16),
            pltpu.VMEM(fitted.shape, BF16),
            pltpu.SemaphoreType.DMA((count * aux // PIECE,)),
        ],
        out_shape=jax.ShapeDtypeStruct(received.shape, BF16),
        compiler_params=pltpu.CompilerParams(vmem_limit_bytes=VMEM_LIMIT),
        cost_estimate=pl.CostEstimate(
            flops=4 * count * aux * window**3,
            bytes_accessed=2 * count * aux * window**2,
            transcendentals=0,
        ),
        name="mix",
    )(slots, fitted, received)


def halves(pair):
    first = lax.broadcasted_iota(jnp.int32, pair.shape, 1) < pair.shape[1] // 2
    return jnp.where(first, pair, 0.0), jnp.where(first, 0.0, pair)


def folded(pair):
    ob = pair.shape[-1] // 2
    return pair[..., :ob] + pair[..., ob:]


def halo_kernel(slab, rows, terms_ref, low_ref, high_ref, total):
    peers, listed, ob, _ = terms_ref.shape
    total[...] = jnp.zeros_like(total)
    for peer in range(peers):
        for i in range(listed):
            for a in range(2):
                row = rows[peer, a, i]

                @pl.when((row < HALO) | (row >= HALO + slab))
                def _():
                    at = jnp.where(row < HALO, row, row - slab)
                    total[at] += halves(terms_ref[peer, i].astype(F32))[a]

    for ref, start in ((low_ref, 0), (high_ref, HALO)):
        sums = folded(total[start : start + HALO])
        for h in range(HALO // 2):
            ref[h] = jnp.concatenate([sums[h], sums[h + HALO // 2]], axis=1)


def halo_sums(slab, rows, terms):
    ob, lanes = terms.shape[2:]
    shape = jax.ShapeDtypeStruct((HALO // 2, ob, lanes), F32)
    return pl.pallas_call(
        functools.partial(halo_kernel, slab),
        in_specs=[in_smem(), in_vmem()],
        out_specs=[in_vmem(), in_vmem()],
        scratch_shapes=[pltpu.VMEM((2 * HALO, ob, lanes), F32)],
        out_shape=[shape, shape],
        cost_estimate=pl.CostEstimate(flops=0, bytes_accessed=2**19, transcendentals=0),
        name="halo_sums",
    )(rows, terms)


def own_kernel(rows, terms_ref, own_ref, edge_ref, total):
    peers, listed, ob, _ = terms_ref.shape
    slab = own_ref.shape[0]
    total[...] = jnp.zeros_like(total)
    for peer in range(peers):
        for i in range(listed):
            pair = halves(terms_ref[peer, i].astype(F32))
            for a in range(2):
                total[rows[peer, a, i]] += pair[a]
    sums = folded(total[HALO : HALO + slab])
    own_ref[...] = sums
    edge_ref[:HALO] = sums[:HALO]
    edge_ref[HALO:] = sums[slab - HALO :]


def own_sums(slab, rows, terms):
    ob, lanes = terms.shape[2:]
    return pl.pallas_call(
        own_kernel,
        in_specs=[in_smem(), in_vmem()],
        out_specs=[in_vmem(), in_vmem()],
        scratch_shapes=[pltpu.VMEM((slab + 2 * HALO, ob, lanes), F32)],
        out_shape=[
            jax.ShapeDtypeStruct((slab, ob, ob), F32),
            jax.ShapeDtypeStruct((2 * HALO, ob, ob), F32),
        ],
        cost_estimate=pl.CostEstimate(flops=0, bytes_accessed=2**21, transcendentals=0),
        name="own_sums",
    )(rows, terms)


def edge_kernel(own_ref, edge_ref, before_ref, after_ref, out_ref, rows, sems):
    del own_ref
    slab, ob = out_ref.shape[:2]
    copies = []
    for side, (ref, start) in enumerate(((before_ref, 0), (after_ref, slab - HALO))):
        at = pl.ds(side * HALO, HALO)
        for h in range(HALO):
            lanes = slice(h // 2 * ob, (h // 2 + 1) * ob)
            rows[side * HALO + h] = edge_ref[side * HALO + h] + ref[h % 2, :, lanes]
        copies.append(
            pltpu.make_async_copy(rows.at[at], out_ref.at[pl.ds(start, HALO)], sems.at[side])
        )
        copies[-1].start()
    for copy in copies:
        copy.wait()


def add_edges(own, edges, before, after):
    return pl.pallas_call(
        edge_kernel,
        in_specs=[pl.BlockSpec(memory_space=pl.ANY), in_vmem(), in_vmem(), in_vmem()],
        out_specs=pl.BlockSpec(memory_space=pl.ANY),
        out_shape=jax.ShapeDtypeStruct(own.shape, F32),
        scratch_shapes=[pltpu.VMEM(edges.shape, F32), pltpu.SemaphoreType.DMA((2,))],
        input_output_aliases={0: 0},
        name="add_edges",
    )(own, edges, before, after)


def ring(value, axis, steps):
    count = lax.axis_size(axis)
    pairs = [(source, (source + steps) % count) for source in range(count)]
    return lax.ppermute(value, axis, pairs)


def per_device(raw_integrals, metric, aux_list, density_list, density_blocks):
    slab, _, ob = density_blocks.shape[:3]
    count, listed = aux_list.shape
    peers = lax.axis_size("dev")
    block_count = slab * lax.axis_size("ta")
    first = lax.axis_index("ta") * slab - HALO
    own = density_blocks.reshape(slab, ob, ob)

    names = jnp.broadcast_to(aux_list[None], (peers, count, listed))
    names = lax.all_to_all(names, "dev", 0, 0, tiled=True)

    rows = (names - first) % block_count
    before = ring(own[-HALO:], "ta", 1)
    after = ring(own[:HALO], "ta", -1)

    packed = pack(rows, own, before, after)
    received = lax.all_to_all(packed, "dev", 0, 0, tiled=True)
    fitted, slots = fit(aux_list, density_list.T, metric, raw_integrals, listed * ob)
    terms = mix(slots, fitted, received)
    terms = lax.all_to_all(terms, "dev", 0, 0, tiled=True)
    low, high = halo_sums(slab, rows, terms)
    from_before = ring(high, "ta", 1)
    from_after = ring(low, "ta", -1)
    totals, edges = own_sums(slab, rows, terms)
    return add_edges(totals, edges, from_before, from_after).reshape(density_blocks.shape)


def solution(mesh):
    placed = (
        P(("ta", "dev"), None, None),
        P(("ta", "dev"), None, None),
        P(("ta", "dev"), None),
        P(),
        P("ta", "dev", None, None),
    )
    return jax.shard_map(
        per_device,
        mesh=mesh,
        in_specs=placed,
        out_specs=P("ta", "dev", None, None),
        check_vma=False,
    )
```

```python
import functools

import jax
import jax.numpy as jnp
from jax import lax
from jax.experimental import pallas as pl
from jax.experimental.pallas import tpu as pltpu
from jax.sharding import PartitionSpec as P

BF16 = jnp.bfloat16
F32 = jnp.float32
HALO = 4
PAIRS = 32
STEP = 32
DEPTH = 3
PIECE = 16
PARTS = ((16, 16, 32), (32, 32))
VMEM_LIMIT = 56 * 2**20


def in_vmem():
    return pl.BlockSpec(memory_space=pltpu.VMEM)


def in_smem():
    return pl.BlockSpec(memory_space=pltpu.SMEM)


def held_in_vmem(value):
    return pltpu.with_memory_space_constraint(value, pltpu.VMEM)


def anywhere():
    return pl.BlockSpec(memory_space=pl.ANY)


def fit_kernel(pairs, stride, names, columns_ref, metric_ref, raw_ref, out_ref, slots, *refs):
    held, made, in_sems, out_sems, columns, listing, *parts = refs
    count, aux = metric_ref.shape[:2]
    rows, width = out_ref.shape[2:]
    pieces = rows // STEP
    total = count * pieces
    chunks = count * rows // pairs

    def arriving(k):
        slot = k % DEPTH
        lanes = pl.ds(k % pieces * STEP * width, STEP * width)
        there = raw_ref.at[k // pieces, :, lanes]
        return pltpu.make_async_copy(there, held.at[slot], in_sems.at[slot])

    def leaving(n):
        a, start = divmod(n * pairs, rows)
        there = out_ref.at[a, :, pl.ds(start, pairs), :]
        return pltpu.make_async_copy(made.at[n % 2], there, out_sems.at[n % 2])

    for k in range(DEPTH):
        arriving(k).start()
    lists = pltpu.make_async_copy(columns_ref, columns, listing)
    lists.start()
    for n in range(chunks):
        metric = metric_ref[n * pairs // rows]
        for r in range(pairs):
            k, at = divmod(n * pairs + r, STEP)
            if at == 0:
                arriving(k).wait()
            lanes = pl.ds(at * width, width)
            both = jnp.dot(metric, held[k % DEPTH, :, lanes], preferred_element_type=F32)
            for v, part in enumerate(parts):
                part[pl.ds(r, aux, stride=stride), :] = both[:, v * 128 : (v + 1) * 128]
            if at == STEP - 1 and k + DEPTH < total:
                arriving(k + DEPTH).start()
        if n >= 2:
            leaving(n - 2).wait()
        for v, part in enumerate(parts):
            values = part[...].reshape(aux, stride, 128)[:, :pairs]
            made[n % 2, :, :, v * 128 : (v + 1) * 128] = values.astype(BF16)
        leaving(n).start()
    lists.wait()
    stored, listed = columns.shape[0], names.shape[1]
    for a in range(count):
        for i in range(listed):
            row = names[a, i]
            for j in range(listed):
                column = names[a, j]
                slot = jnp.int32(-1)
                for k in range(stored):
                    slot = jnp.where(columns[k, row] == column, k, slot)
                slots[(a * listed + i) * listed + j] = slot
    for n in range(chunks - 2, chunks):
        leaving(n).wait()


def fit(names, columns, metric, raw, window):
    count, aux, merged = raw.shape
    listed = names.shape[1]
    stride = PAIRS + 4
    width = 2 * window
    return pl.pallas_call(
        functools.partial(fit_kernel, PAIRS, stride),
        in_specs=[in_smem(), anywhere(), in_vmem(), anywhere()],
        out_specs=[anywhere(), in_smem()],
        out_shape=[
            jax.ShapeDtypeStruct((count, aux, window // 2, width), BF16),
            jax.ShapeDtypeStruct((count * listed * listed,), jnp.int32),
        ],
        scratch_shapes=[
            pltpu.VMEM((DEPTH, aux, STEP * width), BF16),
            pltpu.VMEM((2, aux, PAIRS, width), BF16),
            pltpu.SemaphoreType.DMA((DEPTH,)),
            pltpu.SemaphoreType.DMA((2,)),
            pltpu.SMEM(columns.shape, jnp.int32),
            pltpu.SemaphoreType.DMA,
        ]
        + [pltpu.VMEM((aux * stride, 128), F32)] * (width // 128),
        compiler_params=pltpu.CompilerParams(vmem_limit_bytes=VMEM_LIMIT),
        cost_estimate=pl.CostEstimate(
            flops=2 * count * aux * aux * merged,
            bytes_accessed=4 * count * aux * merged,
            transcendentals=0,
        ),
        name="fit",
    )(names, columns, metric, raw)


def pack_kernel(rows_ref, own_ref, before_ref, after_ref, out_ref, near, rows, sems):
    slab = own_ref.shape[0]
    lists = pltpu.make_async_copy(rows_ref, rows, sems.at[0])
    blocks = pltpu.make_async_copy(own_ref, near.at[pl.ds(HALO, slab)], sems.at[1])
    lists.start()
    blocks.start()
    near[:HALO] = before_ref[...]
    near[HALO + slab :] = after_ref[...]
    lists.wait()
    blocks.wait()
    peers, listed = out_ref.shape[:2]
    for peer in range(peers):
        for i in range(listed):
            pair = [near[rows[peer, a, i]] for a in range(2)]
            out_ref[peer, i] = jnp.concatenate(pair, axis=1)


def pack(rows, own, before, after):
    slab, ob = own.shape[:2]
    peers, _, listed = rows.shape
    return pl.pallas_call(
        pack_kernel,
        in_specs=[anywhere(), anywhere(), in_vmem(), in_vmem()],
        out_specs=in_vmem(),
        scratch_shapes=[
            pltpu.VMEM((slab + 2 * HALO, ob, ob), BF16),
            pltpu.SMEM(rows.shape, jnp.int32),
            pltpu.SemaphoreType.DMA((2,)),
        ],
        out_shape=jax.ShapeDtypeStruct((peers, listed, ob, 2 * ob), BF16),
        cost_estimate=pl.CostEstimate(flops=0, bytes_accessed=2**20, transcendentals=0),
        name="pack",
    )(rows, own, held_in_vmem(before), held_in_vmem(after))


def mix_kernel(slots_ref, fit_ref, recv_ref, out_ref, dens, held, slots, sems, listing):
    count, aux, pairs, width = fit_ref.shape
    listed, ob = recv_ref.shape[1:3]
    window = width // 2
    total = count * aux // PIECE

    def arriving(n):
        at = (n * PIECE // aux, pl.ds(n * PIECE % aux, PIECE))
        return pltpu.make_async_copy(fit_ref.at[at], held.at[at], sems.at[n])

    lists = pltpu.make_async_copy(slots_ref, slots, listing)
    lists.start()
    for n in range(DEPTH):
        arriving(n).start()
    out_ref[...] = jnp.zeros_like(out_ref)
    row = lax.broadcasted_iota(jnp.int32, (window, window), 0)
    column = lax.broadcasted_iota(jnp.int32, (window, window), 1)
    turn = (lax.rem(row, 2) * pairs + lax.div(row, 2) == column).astype(BF16)
    across = (((1,), (1,)), ((), ()))
    lists.wait()
    for a in range(count):
        for i in range(listed):
            blocks = []
            for j in range(listed):
                slot = slots[(a * listed + i) * listed + j]
                block = recv_ref[jnp.maximum(slot, 0), i, :, a * ob : (a + 1) * ob]
                blocks.append(jnp.where(slot >= 0, block, jnp.zeros_like(block)))
            dens[a, i * ob : (i + 1) * ob, :] = jnp.concatenate(blocks, axis=1)
    for a in range(count):
        density = dens[a]
        summed = None
        done = 0
        for part in PARTS[a]:
            for n in range((a * aux + done) // PIECE, (a * aux + done + part) // PIECE):
                arriving(n).wait()
                if n + DEPTH < total:
                    arriving(n + DEPTH).start()
            rows = held[a, pl.ds(done, part)]
            fitted = jnp.concatenate([rows[..., :window], rows[..., window:]], axis=1)
            fitted = fitted.reshape(part * window, window)
            mixed = jnp.dot(fitted, density, preferred_element_type=F32).astype(BF16)
            for q in range(part):
                at = slice(q * window, (q + 1) * window)
                term = lax.dot_general(
                    mixed[at], fitted[at], across, preferred_element_type=F32
                )
                summed = term if summed is None else summed + term
            done += part

        half = lax.dot_general(
            summed.astype(BF16), turn, across, preferred_element_type=F32
        ).astype(BF16)
        terms = jnp.dot(turn, half, preferred_element_type=F32).astype(BF16)
        for i in range(listed):
            for j in range(listed):
                slot = slots[(a * listed + i) * listed + j]
                block = terms[i * ob : (i + 1) * ob, j * ob : (j + 1) * ob]

                @pl.when(slot >= 0)
                def _():
                    out_ref[slot, i, :, a * ob : (a + 1) * ob] = block


def mix(slots, fitted, received):
    count, aux, pairs, width = fitted.shape
    window = width // 2
    return pl.pallas_call(
        mix_kernel,
        in_specs=[anywhere(), anywhere(), in_vmem()],
        out_specs=in_vmem(),
        scratch_shapes=[
            pltpu.VMEM((count, window, window), BF16),
            pltpu.VMEM(fitted.shape, BF16),
            pltpu.SMEM(slots.shape, jnp.int32),
            pltpu.SemaphoreType.DMA((count * aux // PIECE,)),
            pltpu.SemaphoreType.DMA,
        ],
        out_shape=jax.ShapeDtypeStruct(received.shape, BF16),
        compiler_params=pltpu.CompilerParams(vmem_limit_bytes=VMEM_LIMIT),
        cost_estimate=pl.CostEstimate(
            flops=4 * count * aux * window**3,
            bytes_accessed=2 * count * aux * window**2,
            transcendentals=0,
        ),
        name="mix",
    )(slots, fitted, held_in_vmem(received))


def halves(pair):
    first = lax.broadcasted_iota(jnp.int32, pair.shape, 1) < pair.shape[1] // 2
    return jnp.where(first, pair, 0.0), jnp.where(first, 0.0, pair)


def folded(pair):
    ob = pair.shape[-1] // 2
    return pair[..., :ob] + pair[..., ob:]


def halo_kernel(slab, rows, terms_ref, low_ref, high_ref, total):
    peers, listed, ob, _ = terms_ref.shape
    total[...] = jnp.zeros_like(total)
    for peer in range(peers):
        for i in range(listed):
            for a in range(2):
                row = rows[peer, a, i]

                @pl.when((row < HALO) | (row >= HALO + slab))
                def _():
                    at = jnp.where(row < HALO, row, row - slab)
                    total[at] += halves(terms_ref[peer, i].astype(F32))[a]

    for ref, start in ((low_ref, 0), (high_ref, HALO)):
        sums = folded(total[start : start + HALO])
        for h in range(HALO // 2):
            ref[h] = jnp.concatenate([sums[h], sums[h + HALO // 2]], axis=1)


def halo_sums(slab, rows, terms):
    ob, lanes = terms.shape[2:]
    shape = jax.ShapeDtypeStruct((HALO // 2, ob, lanes), F32)
    return pl.pallas_call(
        functools.partial(halo_kernel, slab),
        in_specs=[in_smem(), in_vmem()],
        out_specs=[in_vmem(), in_vmem()],
        scratch_shapes=[pltpu.VMEM((2 * HALO, ob, lanes), F32)],
        out_shape=[shape, shape],
        cost_estimate=pl.CostEstimate(flops=0, bytes_accessed=2**19, transcendentals=0),
        name="halo_sums",
    )(rows, held_in_vmem(terms))


def own_kernel(rows, terms_ref, own_ref, edge_ref, total):
    peers, listed, ob, _ = terms_ref.shape
    slab = own_ref.shape[0]
    total[...] = jnp.zeros_like(total)
    for peer in range(peers):
        for i in range(listed):
            pair = halves(terms_ref[peer, i].astype(F32))
            for a in range(2):
                total[rows[peer, a, i]] += pair[a]
    sums = folded(total[HALO : HALO + slab])
    own_ref[...] = sums
    edge_ref[:HALO] = sums[:HALO]
    edge_ref[HALO:] = sums[slab - HALO :]


def own_sums(slab, rows, terms):
    ob, lanes = terms.shape[2:]
    return pl.pallas_call(
        own_kernel,
        in_specs=[in_smem(), in_vmem()],
        out_specs=[in_vmem(), in_vmem()],
        scratch_shapes=[pltpu.VMEM((slab + 2 * HALO, ob, lanes), F32)],
        out_shape=[
            jax.ShapeDtypeStruct((slab, ob, ob), F32),
            jax.ShapeDtypeStruct((2 * HALO, ob, ob), F32),
        ],
        cost_estimate=pl.CostEstimate(flops=0, bytes_accessed=2**21, transcendentals=0),
        name="own_sums",
    )(rows, held_in_vmem(terms))


def edge_kernel(own_ref, edge_ref, before_ref, after_ref, out_ref, rows, sems):
    del own_ref
    slab, ob = out_ref.shape[:2]
    copies = []
    for side, (ref, start) in enumerate(((before_ref, 0), (after_ref, slab - HALO))):
        at = pl.ds(side * HALO, HALO)
        for h in range(HALO):
            lanes = slice(h // 2 * ob, (h // 2 + 1) * ob)
            rows[side * HALO + h] = edge_ref[side * HALO + h] + ref[h % 2, :, lanes]
        copies.append(
            pltpu.make_async_copy(rows.at[at], out_ref.at[pl.ds(start, HALO)], sems.at[side])
        )
        copies[-1].start()
    for copy in copies:
        copy.wait()


def add_edges(own, edges, before, after):
    return pl.pallas_call(
        edge_kernel,
        in_specs=[pl.BlockSpec(memory_space=pl.ANY), in_vmem(), in_vmem(), in_vmem()],
        out_specs=pl.BlockSpec(memory_space=pl.ANY),
        out_shape=jax.ShapeDtypeStruct(own.shape, F32),
        scratch_shapes=[pltpu.VMEM(edges.shape, F32), pltpu.SemaphoreType.DMA((2,))],
        input_output_aliases={0: 0},
        name="add_edges",
    )(own, held_in_vmem(edges), held_in_vmem(before), held_in_vmem(after))


def ring(value, axis, steps):
    count = lax.axis_size(axis)
    pairs = [(source, (source + steps) % count) for source in range(count)]
    return lax.ppermute(value, axis, pairs)


def per_device(raw_integrals, metric, aux_list, density_list, density_blocks):
    slab, _, ob = density_blocks.shape[:3]
    count, listed = aux_list.shape
    peers = lax.axis_size("dev")
    block_count = slab * lax.axis_size("ta")
    first = lax.axis_index("ta") * slab - HALO
    own = density_blocks.reshape(slab, ob, ob)

    names = jnp.broadcast_to(aux_list[None], (peers, count, listed))
    names = lax.all_to_all(names, "dev", 0, 0, tiled=True)

    rows = (names - first) % block_count
    before = ring(own[-HALO:], "ta", 1)
    after = ring(own[:HALO], "ta", -1)

    packed = pack(rows, own, before, after)
    received = lax.all_to_all(packed, "dev", 0, 0, tiled=True)
    fitted, slots = fit(aux_list, density_list.T, metric, raw_integrals, listed * ob)
    terms = mix(slots, fitted, received)
    terms = lax.all_to_all(terms, "dev", 0, 0, tiled=True)
    low, high = halo_sums(slab, rows, terms)
    from_before = ring(high, "ta", 1)
    from_after = ring(low, "ta", -1)
    totals, edges = own_sums(slab, rows, terms)
    return add_edges(totals, edges, from_before, from_after).reshape(density_blocks.shape)


def solution(mesh):
    placed = (
        P(("ta", "dev"), None, None),
        P(("ta", "dev"), None, None),
        P(("ta", "dev"), None),
        P(),
        P("ta", "dev", None, None),
    )
    return jax.shard_map(
        per_device,
        mesh=mesh,
        in_specs=placed,
        out_specs=P("ta", "dev", None, None),
        check_vma=False,
    )
```

```python
import functools

import jax
import jax.numpy as jnp
from jax import lax
from jax.experimental import pallas as pl
from jax.experimental.pallas import tpu as pltpu
from jax.sharding import PartitionSpec as P

BF16 = jnp.bfloat16
F32 = jnp.float32
HALO = 4
PAIRS = 32
STEP = 32
DEPTH = 3
PIECE = 16
MDEPTH = 8
PARTS = ((16, 16, 32), (32, 32))
VMEM_LIMIT = 56 * 2**20


def in_vmem():
    return pl.BlockSpec(memory_space=pltpu.VMEM)


def in_smem():
    return pl.BlockSpec(memory_space=pltpu.SMEM)


def held_in_vmem(value):
    return pltpu.with_memory_space_constraint(value, pltpu.VMEM)


def anywhere():
    return pl.BlockSpec(memory_space=pl.ANY)


def fit_kernel(pairs, stride, names, columns_ref, metric_ref, raw_ref, out_ref, slots, *refs):
    held, made, in_sems, out_sems, columns, listing, *parts = refs
    count, aux = metric_ref.shape[:2]
    rows, width = out_ref.shape[2:]
    pieces = rows // STEP
    total = count * pieces
    chunks = count * rows // pairs

    def arriving(k):
        slot = k % DEPTH
        lanes = pl.ds(k % pieces * STEP * width, STEP * width)
        there = raw_ref.at[k // pieces, :, lanes]
        return pltpu.make_async_copy(there, held.at[slot], in_sems.at[slot])

    def leaving(n):
        a, start = divmod(n * pairs, rows)
        there = out_ref.at[a, :, pl.ds(start, pairs), :]
        return pltpu.make_async_copy(made.at[n % 2], there, out_sems.at[n % 2])

    for k in range(DEPTH):
        arriving(k).start()
    lists = pltpu.make_async_copy(columns_ref, columns, listing)
    lists.start()
    for n in range(chunks):
        metric = metric_ref[n * pairs // rows]
        for r in range(pairs):
            k, at = divmod(n * pairs + r, STEP)
            if at == 0:
                arriving(k).wait()
            lanes = pl.ds(at * width, width)
            both = jnp.dot(metric, held[k % DEPTH, :, lanes], preferred_element_type=F32)
            for v, part in enumerate(parts):
                part[pl.ds(r, aux, stride=stride), :] = both[:, v * 128 : (v + 1) * 128]
            if at == STEP - 1 and k + DEPTH < total:
                arriving(k + DEPTH).start()
        if n >= 2:
            leaving(n - 2).wait()
        for v, part in enumerate(parts):
            values = part[...].reshape(aux, stride, 128)[:, :pairs]
            made[n % 2, :, :, v * 128 : (v + 1) * 128] = values.astype(BF16)
        leaving(n).start()
    lists.wait()
    stored, listed = columns.shape[0], names.shape[1]
    for a in range(count):
        for i in range(listed):
            row = names[a, i]
            for j in range(listed):
                column = names[a, j]
                slot = jnp.int32(-1)
                for k in range(stored):
                    slot = jnp.where(columns[k, row] == column, k, slot)
                slots[(a * listed + i) * listed + j] = slot
    for n in range(chunks - 2, chunks):
        leaving(n).wait()


def fit(names, columns, metric, raw, window):
    count, aux, merged = raw.shape
    listed = names.shape[1]
    stride = PAIRS + 4
    width = 2 * window
    return pl.pallas_call(
        functools.partial(fit_kernel, PAIRS, stride),
        in_specs=[in_smem(), anywhere(), in_vmem(), anywhere()],
        out_specs=[anywhere(), in_smem()],
        out_shape=[
            jax.ShapeDtypeStruct((count, aux, window // 2, width), BF16),
            jax.ShapeDtypeStruct((count * listed * listed,), jnp.int32),
        ],
        scratch_shapes=[
            pltpu.VMEM((DEPTH, aux, STEP * width), BF16),
            pltpu.VMEM((2, aux, PAIRS, width), BF16),
            pltpu.SemaphoreType.DMA((DEPTH,)),
            pltpu.SemaphoreType.DMA((2,)),
            pltpu.SMEM(columns.shape, jnp.int32),
            pltpu.SemaphoreType.DMA,
        ]
        + [pltpu.VMEM((aux * stride, 128), F32)] * (width // 128),
        compiler_params=pltpu.CompilerParams(vmem_limit_bytes=VMEM_LIMIT),
        cost_estimate=pl.CostEstimate(
            flops=2 * count * aux * aux * merged,
            bytes_accessed=4 * count * aux * merged,
            transcendentals=0,
        ),
        name="fit",
    )(names, columns, metric, raw)


def pack_kernel(rows_ref, own_ref, before_ref, after_ref, out_ref, near, rows, sems):
    slab = own_ref.shape[0]
    lists = pltpu.make_async_copy(rows_ref, rows, sems.at[0])
    blocks = pltpu.make_async_copy(own_ref, near.at[pl.ds(HALO, slab)], sems.at[1])
    lists.start()
    blocks.start()
    near[:HALO] = before_ref[...]
    near[HALO + slab :] = after_ref[...]
    lists.wait()
    blocks.wait()
    peers, listed = out_ref.shape[:2]
    for peer in range(peers):
        for i in range(listed):
            pair = [near[rows[peer, a, i]] for a in range(2)]
            out_ref[peer, i] = jnp.concatenate(pair, axis=1)


def pack(rows, own, before, after):
    slab, ob = own.shape[:2]
    peers, _, listed = rows.shape
    return pl.pallas_call(
        pack_kernel,
        in_specs=[anywhere(), anywhere(), in_vmem(), in_vmem()],
        out_specs=in_vmem(),
        scratch_shapes=[
            pltpu.VMEM((slab + 2 * HALO, ob, ob), BF16),
            pltpu.SMEM(rows.shape, jnp.int32),
            pltpu.SemaphoreType.DMA((2,)),
        ],
        out_shape=jax.ShapeDtypeStruct((peers, listed, ob, 2 * ob), BF16),
        cost_estimate=pl.CostEstimate(flops=0, bytes_accessed=2**20, transcendentals=0),
        name="pack",
    )(rows, own, held_in_vmem(before), held_in_vmem(after))


def mix_kernel(slots_ref, fit_ref, recv_ref, out_ref, dens, made, held, slots, sems, listing):
    count, aux, pairs, width = fit_ref.shape
    listed, ob = recv_ref.shape[1:3]
    window = width // 2
    total = count * aux // PIECE

    def arriving(n):
        at = (n * PIECE // aux, pl.ds(n * PIECE % aux, PIECE))
        return pltpu.make_async_copy(fit_ref.at[at], held.at[at], sems.at[n])

    lists = pltpu.make_async_copy(slots_ref, slots, listing)
    lists.start()
    for n in range(MDEPTH):
        arriving(n).start()
    made[...] = jnp.zeros_like(made)
    row = lax.broadcasted_iota(jnp.int32, (window, window), 0)
    column = lax.broadcasted_iota(jnp.int32, (window, window), 1)
    turn = ((row & 1) * pairs + (row >> 1) == column).astype(BF16)
    across = (((1,), (1,)), ((), ()))
    lists.wait()
    sums = []
    for a in range(count):
        for i in range(listed):
            blocks = []
            for j in range(listed):
                slot = slots[(a * listed + i) * listed + j]
                block = recv_ref[jnp.maximum(slot, 0), i, :, a * ob : (a + 1) * ob]
                blocks.append(jnp.where(slot >= 0, block, jnp.zeros_like(block)))
            dens[a, i * ob : (i + 1) * ob, :] = jnp.concatenate(blocks, axis=1)
    for a in range(count):
        density = dens[a]
        summed = None
        done = 0
        for part in PARTS[a]:
            for n in range((a * aux + done) // PIECE, (a * aux + done + part) // PIECE):
                arriving(n).wait()
                if n + MDEPTH < total:
                    arriving(n + MDEPTH).start()
            rows = held[a, pl.ds(done, part)]
            fitted = jnp.concatenate([rows[..., :window], rows[..., window:]], axis=1)
            fitted = fitted.reshape(part * window, window)
            mixed = jnp.dot(fitted, density, preferred_element_type=F32).astype(BF16)
            for q in range(part):
                at = slice(q * window, (q + 1) * window)
                term = lax.dot_general(
                    mixed[at], fitted[at], across, preferred_element_type=F32
                )
                summed = term if summed is None else summed + term
            done += part

        sums.append(summed.astype(BF16))

    halfs = [lax.dot_general(x, turn, across, preferred_element_type=F32).astype(BF16) for x in sums]
    terms = [jnp.dot(turn, x, preferred_element_type=F32).astype(BF16) for x in halfs]
    for a in range(count):
        for i in range(listed):
            for j in range(listed):
                slot = slots[(a * listed + i) * listed + j]
                at = jnp.where(slot >= 0, slot, out_ref.shape[0])
                block = terms[a][i * ob : (i + 1) * ob, j * ob : (j + 1) * ob]
                made[at, i, :, a * ob : (a + 1) * ob] = block
    out_ref[...] = made[: out_ref.shape[0]]


def mix(slots, fitted, received):
    count, aux, pairs, width = fitted.shape
    window = width // 2
    return pl.pallas_call(
        mix_kernel,
        in_specs=[anywhere(), anywhere(), in_vmem()],
        out_specs=in_vmem(),
        scratch_shapes=[
            pltpu.VMEM((count, window, window), BF16),
            pltpu.VMEM((received.shape[0] + 1,) + received.shape[1:], BF16),
            pltpu.VMEM(fitted.shape, BF16),
            pltpu.SMEM(slots.shape, jnp.int32),
            pltpu.SemaphoreType.DMA((count * aux // PIECE,)),
            pltpu.SemaphoreType.DMA,
        ],
        out_shape=jax.ShapeDtypeStruct(received.shape, BF16),
        compiler_params=pltpu.CompilerParams(vmem_limit_bytes=VMEM_LIMIT),
        cost_estimate=pl.CostEstimate(
            flops=4 * count * aux * window**3,
            bytes_accessed=2 * count * aux * window**2,
            transcendentals=0,
        ),
        name="mix",
    )(slots, fitted, held_in_vmem(received))


def halves(pair):
    first = lax.broadcasted_iota(jnp.int32, pair.shape, 1) < pair.shape[1] // 2
    return jnp.where(first, pair, 0.0), jnp.where(first, 0.0, pair)


def folded(pair):
    ob = pair.shape[-1] // 2
    return pair[..., :ob] + pair[..., ob:]


def halo_kernel(slab, rows, terms_ref, low_ref, high_ref, total):
    peers, listed, ob, _ = terms_ref.shape
    total[...] = jnp.zeros_like(total)
    for peer in range(peers):
        for i in range(listed):
            pair = halves(terms_ref[peer, i].astype(F32))
            for a in range(2):
                row = rows[peer, a, i]
                other = jnp.where(row < HALO + slab, 2 * HALO + a, row - slab)
                total[jnp.where(row < HALO, row, other)] += pair[a]

    for ref, start in ((low_ref, 0), (high_ref, HALO)):
        sums = folded(total[start : start + HALO])
        for h in range(HALO // 2):
            ref[h] = jnp.concatenate([sums[h], sums[h + HALO // 2]], axis=1)


def halo_sums(slab, rows, terms):
    ob, lanes = terms.shape[2:]
    shape = jax.ShapeDtypeStruct((HALO // 2, ob, lanes), F32)
    return pl.pallas_call(
        functools.partial(halo_kernel, slab),
        in_specs=[in_smem(), in_vmem()],
        out_specs=[in_vmem(), in_vmem()],
        scratch_shapes=[pltpu.VMEM((2 * HALO + 2, ob, lanes), F32)],
        out_shape=[shape, shape],
        cost_estimate=pl.CostEstimate(flops=0, bytes_accessed=2**19, transcendentals=0),
        name="halo_sums",
    )(rows, held_in_vmem(terms))


def own_kernel(rows, terms_ref, own_ref, edge_ref, total):
    peers, listed, ob, _ = terms_ref.shape
    slab = own_ref.shape[0]
    total[...] = jnp.zeros_like(total)
    for peer in range(peers):
        for i in range(listed):
            pair = halves(terms_ref[peer, i].astype(F32))
            for a in range(2):
                total[rows[peer, a, i]] += pair[a]
    sums = folded(total[HALO : HALO + slab])
    own_ref[...] = sums
    edge_ref[:HALO] = sums[:HALO]
    edge_ref[HALO:] = sums[slab - HALO :]


def own_sums(slab, rows, terms):
    ob, lanes = terms.shape[2:]
    return pl.pallas_call(
        own_kernel,
        in_specs=[in_smem(), in_vmem()],
        out_specs=[in_vmem(), in_vmem()],
        scratch_shapes=[pltpu.VMEM((slab + 2 * HALO, ob, lanes), F32)],
        out_shape=[
            jax.ShapeDtypeStruct((slab, ob, ob), F32),
            jax.ShapeDtypeStruct((2 * HALO, ob, ob), F32),
        ],
        cost_estimate=pl.CostEstimate(flops=0, bytes_accessed=2**21, transcendentals=0),
        name="own_sums",
    )(rows, held_in_vmem(terms))


def edge_kernel(own_ref, edge_ref, before_ref, after_ref, out_ref, rows, sems):
    del own_ref
    slab, ob = out_ref.shape[:2]
    copies = []
    for side, (ref, start) in enumerate(((before_ref, 0), (after_ref, slab - HALO))):
        at = pl.ds(side * HALO, HALO)
        for h in range(HALO):
            lanes = slice(h // 2 * ob, (h // 2 + 1) * ob)
            rows[side * HALO + h] = edge_ref[side * HALO + h] + ref[h % 2, :, lanes]
        copies.append(
            pltpu.make_async_copy(rows.at[at], out_ref.at[pl.ds(start, HALO)], sems.at[side])
        )
        copies[-1].start()
    for copy in copies:
        copy.wait()


def add_edges(own, edges, before, after):
    return pl.pallas_call(
        edge_kernel,
        in_specs=[pl.BlockSpec(memory_space=pl.ANY), in_vmem(), in_vmem(), in_vmem()],
        out_specs=pl.BlockSpec(memory_space=pl.ANY),
        out_shape=jax.ShapeDtypeStruct(own.shape, F32),
        scratch_shapes=[pltpu.VMEM(edges.shape, F32), pltpu.SemaphoreType.DMA((2,))],
        input_output_aliases={0: 0},
        name="add_edges",
    )(own, held_in_vmem(edges), held_in_vmem(before), held_in_vmem(after))


def ring(value, axis, steps):
    count = lax.axis_size(axis)
    pairs = [(source, (source + steps) % count) for source in range(count)]
    return lax.ppermute(value, axis, pairs)


def per_device(raw_integrals, metric, aux_list, density_list, density_blocks):
    slab, _, ob = density_blocks.shape[:3]
    count, listed = aux_list.shape
    peers = lax.axis_size("dev")
    block_count = slab * lax.axis_size("ta")
    first = lax.axis_index("ta") * slab - HALO
    own = density_blocks.reshape(slab, ob, ob)

    names = jnp.broadcast_to(aux_list[None], (peers, count, listed))
    names = lax.all_to_all(names, "dev", 0, 0, tiled=True)

    rows = (names - first) % block_count
    before = ring(own[-HALO:], "ta", 1)
    after = ring(own[:HALO], "ta", -1)

    packed = pack(rows, own, before, after)
    received = lax.all_to_all(packed, "dev", 0, 0, tiled=True)
    fitted, slots = fit(aux_list, density_list.T, metric, raw_integrals, listed * ob)
    terms = mix(slots, fitted, received)
    terms = lax.all_to_all(terms, "dev", 0, 0, tiled=True)
    low, high = halo_sums(slab, rows, terms)
    from_before = ring(high, "ta", 1)
    from_after = ring(low, "ta", -1)
    totals, edges = own_sums(slab, rows, terms)
    return add_edges(totals, edges, from_before, from_after).reshape(density_blocks.shape)


def solution(mesh):
    placed = (
        P(("ta", "dev"), None, None),
        P(("ta", "dev"), None, None),
        P(("ta", "dev"), None),
        P(),
        P("ta", "dev", None, None),
    )
    return jax.shard_map(
        per_device,
        mesh=mesh,
        in_specs=placed,
        out_specs=P("ta", "dev", None, None),
        check_vma=False,
    )
```

```python
import functools

import jax
import jax.numpy as jnp
from jax import lax
from jax.experimental import pallas as pl
from jax.experimental.pallas import tpu as pltpu
from jax.sharding import PartitionSpec as P

BF16 = jnp.bfloat16
F32 = jnp.float32
HALO = 4
PAIRS = 32
STEP = 32
DEPTH = 3
PIECE = 16
MDEPTH = 8
PARTS = ((16, 16, 32), (32, 32))
VMEM_LIMIT = 56 * 2**20


def in_vmem():
    return pl.BlockSpec(memory_space=pltpu.VMEM)


def in_smem():
    return pl.BlockSpec(memory_space=pltpu.SMEM)


def held_in_vmem(value):
    return pltpu.with_memory_space_constraint(value, pltpu.VMEM)


def anywhere():
    return pl.BlockSpec(memory_space=pl.ANY)


def fit_kernel(pairs, stride, names, columns_ref, metric_ref, raw_ref, out_ref, slots, *refs):
    held, made, in_sems, out_sems, columns, listing, *parts = refs
    count, aux = metric_ref.shape[:2]
    rows, width = out_ref.shape[2:]
    pieces = rows // STEP
    total = count * pieces
    chunks = count * rows // pairs

    def arriving(k):
        slot = k % DEPTH
        lanes = pl.ds(k % pieces * STEP * width, STEP * width)
        there = raw_ref.at[k // pieces, :, lanes]
        return pltpu.make_async_copy(there, held.at[slot], in_sems.at[slot])

    def leaving(n):
        a, start = divmod(n * pairs, rows)
        there = out_ref.at[a, :, pl.ds(start, pairs), :]
        return pltpu.make_async_copy(made.at[n % 2], there, out_sems.at[n % 2])

    for k in range(DEPTH):
        arriving(k).start()
    lists = pltpu.make_async_copy(columns_ref, columns, listing)
    lists.start()
    for n in range(chunks):
        metric = metric_ref[n * pairs // rows]
        for r in range(pairs):
            k, at = divmod(n * pairs + r, STEP)
            if at == 0:
                arriving(k).wait()
            lanes = pl.ds(at * width, width)
            both = jnp.dot(metric, held[k % DEPTH, :, lanes], preferred_element_type=F32)
            for v, part in enumerate(parts):
                part[pl.ds(r, aux, stride=stride), :] = both[:, v * 128 : (v + 1) * 128]
            if at == STEP - 1 and k + DEPTH < total:
                arriving(k + DEPTH).start()
        if n >= 2:
            leaving(n - 2).wait()
        for v, part in enumerate(parts):
            values = part[: aux * stride].reshape(aux, stride, 128)[:, :pairs]
            made[n % 2, :, :, v * 128 : (v + 1) * 128] = values.astype(BF16)
        leaving(n).start()
    lists.wait()
    stored, listed = columns.shape[0], names.shape[1]
    for a in range(count):
        for i in range(listed):
            row = names[a, i]
            for j in range(listed):
                column = names[a, j]
                slot = jnp.int32(-1)
                for k in range(stored):
                    slot = jnp.where(columns[k, row] == column, k, slot)
                slots[(a * listed + i) * listed + j] = slot
    for n in range(chunks - 2, chunks):
        leaving(n).wait()


def fit(names, columns, metric, raw, window):
    count, aux, merged = raw.shape
    listed = names.shape[1]
    stride = PAIRS + 4
    width = 2 * window
    return pl.pallas_call(
        functools.partial(fit_kernel, PAIRS, stride),
        in_specs=[in_smem(), anywhere(), in_vmem(), anywhere()],
        out_specs=[anywhere(), in_smem()],
        out_shape=[
            jax.ShapeDtypeStruct((count, aux, window // 2, width), BF16),
            jax.ShapeDtypeStruct((count * listed * listed,), jnp.int32),
        ],
        scratch_shapes=[
            pltpu.VMEM((DEPTH, aux, STEP * width), BF16),
            pltpu.VMEM((2, aux, PAIRS, width), BF16),
            pltpu.SemaphoreType.DMA((DEPTH,)),
            pltpu.SemaphoreType.DMA((2,)),
            pltpu.SMEM(columns.shape, jnp.int32),
            pltpu.SemaphoreType.DMA,
        ]
        + [pltpu.VMEM(((aux + 1) * stride, 128), F32)] * (width // 128),
        compiler_params=pltpu.CompilerParams(vmem_limit_bytes=VMEM_LIMIT),
        cost_estimate=pl.CostEstimate(
            flops=2 * count * aux * aux * merged,
            bytes_accessed=4 * count * aux * merged,
            transcendentals=0,
        ),
        name="fit",
    )(names, columns, metric, raw)


def pack_kernel(rows_ref, own_ref, before_ref, after_ref, out_ref, near, rows, sems):
    slab = own_ref.shape[0]
    lists = pltpu.make_async_copy(rows_ref, rows, sems.at[0])
    blocks = pltpu.make_async_copy(own_ref, near.at[pl.ds(HALO, slab)], sems.at[1])
    lists.start()
    blocks.start()
    near[:HALO] = before_ref[...]
    near[HALO + slab :] = after_ref[...]
    lists.wait()
    blocks.wait()
    peers, listed = out_ref.shape[:2]
    for peer in range(peers):
        for i in range(listed):
            pair = [near[rows[peer, a, i]] for a in range(2)]
            out_ref[peer, i] = jnp.concatenate(pair, axis=1)


def pack(rows, own, before, after):
    slab, ob = own.shape[:2]
    peers, _, listed = rows.shape
    return pl.pallas_call(
        pack_kernel,
        in_specs=[anywhere(), anywhere(), in_vmem(), in_vmem()],
        out_specs=in_vmem(),
        scratch_shapes=[
            pltpu.VMEM((slab + 2 * HALO, ob, ob), BF16),
            pltpu.SMEM(rows.shape, jnp.int32),
            pltpu.SemaphoreType.DMA((2,)),
        ],
        out_shape=jax.ShapeDtypeStruct((peers, listed, ob, 2 * ob), BF16),
        cost_estimate=pl.CostEstimate(flops=0, bytes_accessed=2**20, transcendentals=0),
        name="pack",
    )(rows, own, held_in_vmem(before), held_in_vmem(after))


def mix_kernel(slots_ref, fit_ref, recv_ref, out_ref, dens, made, held, slots, sems, listing):
    count, aux, pairs, width = fit_ref.shape
    listed, ob = recv_ref.shape[1:3]
    window = width // 2
    total = count * aux // PIECE

    def arriving(n):
        at = (n * PIECE // aux, pl.ds(n * PIECE % aux, PIECE))
        return pltpu.make_async_copy(fit_ref.at[at], held.at[at], sems.at[n])

    lists = pltpu.make_async_copy(slots_ref, slots, listing)
    lists.start()
    for n in range(MDEPTH):
        arriving(n).start()
    made[...] = jnp.zeros_like(made)
    row = lax.broadcasted_iota(jnp.int32, (window, window), 0)
    column = lax.broadcasted_iota(jnp.int32, (window, window), 1)
    turn = ((row & 1) * pairs + (row >> 1) == column).astype(BF16)
    across = (((1,), (1,)), ((), ()))
    lists.wait()
    sums = []
    for a in range(count):
        for i in range(listed):
            blocks = []
            for j in range(listed):
                slot = slots[(a * listed + i) * listed + j]
                block = recv_ref[jnp.maximum(slot, 0), i, :, a * ob : (a + 1) * ob]
                blocks.append(jnp.where(slot >= 0, block, jnp.zeros_like(block)))
            dens[a, i * ob : (i + 1) * ob, :] = jnp.concatenate(blocks, axis=1)
    for a in range(count):
        density = dens[a]
        summed = None
        done = 0
        for part in PARTS[a]:
            for n in range((a * aux + done) // PIECE, (a * aux + done + part) // PIECE):
                arriving(n).wait()
                if n + MDEPTH < total:
                    arriving(n + MDEPTH).start()
            rows = held[a, pl.ds(done, part)]
            fitted = jnp.concatenate([rows[..., :window], rows[..., window:]], axis=1)
            fitted = fitted.reshape(part * window, window)
            mixed = jnp.dot(fitted, density, preferred_element_type=F32).astype(BF16)
            for q in range(part):
                at = slice(q * window, (q + 1) * window)
                term = lax.dot_general(
                    mixed[at], fitted[at], across, preferred_element_type=F32
                )
                summed = term if summed is None else summed + term
            done += part

        sums.append(summed.astype(BF16))

    halfs = [lax.dot_general(x, turn, across, preferred_element_type=F32).astype(BF16) for x in sums]
    terms = [jnp.dot(turn, x, preferred_element_type=F32).astype(BF16) for x in halfs]
    for a in range(count):
        for i in range(listed):
            for j in range(listed):
                slot = slots[(a * listed + i) * listed + j]
                at = jnp.where(slot >= 0, slot, out_ref.shape[0])
                block = terms[a][i * ob : (i + 1) * ob, j * ob : (j + 1) * ob]
                made[at, i, :, a * ob : (a + 1) * ob] = block
    out_ref[...] = made[: out_ref.shape[0]]


def mix(slots, fitted, received):
    count, aux, pairs, width = fitted.shape
    window = width // 2
    return pl.pallas_call(
        mix_kernel,
        in_specs=[anywhere(), anywhere(), in_vmem()],
        out_specs=in_vmem(),
        scratch_shapes=[
            pltpu.VMEM((count, window, window), BF16),
            pltpu.VMEM((received.shape[0] + 1,) + received.shape[1:], BF16),
            pltpu.VMEM(fitted.shape, BF16),
            pltpu.SMEM(slots.shape, jnp.int32),
            pltpu.SemaphoreType.DMA((count * aux // PIECE,)),
            pltpu.SemaphoreType.DMA,
        ],
        out_shape=jax.ShapeDtypeStruct(received.shape, BF16),
        compiler_params=pltpu.CompilerParams(vmem_limit_bytes=VMEM_LIMIT),
        cost_estimate=pl.CostEstimate(
            flops=4 * count * aux * window**3,
            bytes_accessed=2 * count * aux * window**2,
            transcendentals=0,
        ),
        name="mix",
    )(slots, fitted, held_in_vmem(received))


def halves(pair):
    first = lax.broadcasted_iota(jnp.int32, pair.shape, 1) < pair.shape[1] // 2
    return jnp.where(first, pair, 0.0), jnp.where(first, 0.0, pair)


def folded(pair):
    ob = pair.shape[-1] // 2
    return pair[..., :ob] + pair[..., ob:]


def halo_kernel(slab, rows, terms_ref, low_ref, high_ref, total):
    peers, listed, ob, _ = terms_ref.shape
    total[...] = jnp.zeros_like(total)
    for peer in range(peers):
        for i in range(listed):
            pair = halves(terms_ref[peer, i].astype(F32))
            for a in range(2):
                row = rows[peer, a, i]
                other = jnp.where(row < HALO + slab, 2 * HALO + a, row - slab)
                total[jnp.where(row < HALO, row, other)] += pair[a]

    for ref, start in ((low_ref, 0), (high_ref, HALO)):
        sums = folded(total[start : start + HALO])
        for h in range(HALO // 2):
            ref[h] = jnp.concatenate([sums[h], sums[h + HALO // 2]], axis=1)


def halo_sums(slab, rows, terms):
    ob, lanes = terms.shape[2:]
    shape = jax.ShapeDtypeStruct((HALO // 2, ob, lanes), F32)
    return pl.pallas_call(
        functools.partial(halo_kernel, slab),
        in_specs=[in_smem(), in_vmem()],
        out_specs=[in_vmem(), in_vmem()],
        scratch_shapes=[pltpu.VMEM((2 * HALO + 2, ob, lanes), F32)],
        out_shape=[shape, shape],
        cost_estimate=pl.CostEstimate(flops=0, bytes_accessed=2**19, transcendentals=0),
        name="halo_sums",
    )(rows, held_in_vmem(terms))


def own_kernel(rows, terms_ref, own_ref, edge_ref, total):
    peers, listed, ob, _ = terms_ref.shape
    slab = own_ref.shape[0]
    total[...] = jnp.zeros_like(total)
    for peer in range(peers):
        for i in range(listed):
            pair = halves(terms_ref[peer, i].astype(F32))
            for a in range(2):
                total[rows[peer, a, i]] += pair[a]
    sums = folded(total[HALO : HALO + slab])
    own_ref[...] = sums
    edge_ref[:HALO] = sums[:HALO]
    edge_ref[HALO:] = sums[slab - HALO :]


def own_sums(slab, rows, terms):
    ob, lanes = terms.shape[2:]
    return pl.pallas_call(
        own_kernel,
        in_specs=[in_smem(), in_vmem()],
        out_specs=[in_vmem(), in_vmem()],
        scratch_shapes=[pltpu.VMEM((slab + 2 * HALO, ob, lanes), F32)],
        out_shape=[
            jax.ShapeDtypeStruct((slab, ob, ob), F32),
            jax.ShapeDtypeStruct((2 * HALO, ob, ob), F32),
        ],
        cost_estimate=pl.CostEstimate(flops=0, bytes_accessed=2**21, transcendentals=0),
        name="own_sums",
    )(rows, held_in_vmem(terms))


def edge_kernel(own_ref, edge_ref, before_ref, after_ref, out_ref, rows, sems):
    del own_ref
    slab, ob = out_ref.shape[:2]
    copies = []
    for side, (ref, start) in enumerate(((before_ref, 0), (after_ref, slab - HALO))):
        at = pl.ds(side * HALO, HALO)
        for h in range(HALO):
            lanes = slice(h // 2 * ob, (h // 2 + 1) * ob)
            rows[side * HALO + h] = edge_ref[side * HALO + h] + ref[h % 2, :, lanes]
        copies.append(
            pltpu.make_async_copy(rows.at[at], out_ref.at[pl.ds(start, HALO)], sems.at[side])
        )
        copies[-1].start()
    for copy in copies:
        copy.wait()


def add_edges(own, edges, before, after):
    return pl.pallas_call(
        edge_kernel,
        in_specs=[pl.BlockSpec(memory_space=pl.ANY), in_vmem(), in_vmem(), in_vmem()],
        out_specs=pl.BlockSpec(memory_space=pl.ANY),
        out_shape=jax.ShapeDtypeStruct(own.shape, F32),
        scratch_shapes=[pltpu.VMEM(edges.shape, F32), pltpu.SemaphoreType.DMA((2,))],
        input_output_aliases={0: 0},
        name="add_edges",
    )(own, held_in_vmem(edges), held_in_vmem(before), held_in_vmem(after))


def ring(value, axis, steps):
    count = lax.axis_size(axis)
    pairs = [(source, (source + steps) % count) for source in range(count)]
    return lax.ppermute(value, axis, pairs)


def per_device(raw_integrals, metric, aux_list, density_list, density_blocks):
    slab, _, ob = density_blocks.shape[:3]
    count, listed = aux_list.shape
    peers = lax.axis_size("dev")
    block_count = slab * lax.axis_size("ta")
    first = lax.axis_index("ta") * slab - HALO
    own = density_blocks.reshape(slab, ob, ob)

    names = jnp.broadcast_to(aux_list[None], (peers, count, listed))
    names = lax.all_to_all(names, "dev", 0, 0, tiled=True)

    rows = (names - first) % block_count
    before = ring(own[-HALO:], "ta", 1)
    after = ring(own[:HALO], "ta", -1)

    packed = pack(rows, own, before, after)
    received = lax.all_to_all(packed, "dev", 0, 0, tiled=True)
    fitted, slots = fit(aux_list, density_list.T, metric, raw_integrals, listed * ob)
    terms = mix(slots, fitted, received)
    terms = lax.all_to_all(terms, "dev", 0, 0, tiled=True)
    low, high = halo_sums(slab, rows, terms)
    from_before = ring(high, "ta", 1)
    from_after = ring(low, "ta", -1)
    totals, edges = own_sums(slab, rows, terms)
    return add_edges(totals, edges, from_before, from_after).reshape(density_blocks.shape)


def solution(mesh):
    placed = (
        P(("ta", "dev"), None, None),
        P(("ta", "dev"), None, None),
        P(("ta", "dev"), None),
        P(),
        P("ta", "dev", None, None),
    )
    return jax.shard_map(
        per_device,
        mesh=mesh,
        in_specs=placed,
        out_specs=P("ta", "dev", None, None),
        check_vma=False,
    )
```
